32 devices in a mesh: dp: 8 (over z, x), section: 4 (over y, core).
Axes of the slice: x: 2, y: 2, z: 4, core: 2. Of those that a mesh axis runs over, the one named last changes fastest.
Arguments:
- acts: bfloat16 [4, 8, 512, 256], P('section', 'dp'), may hold values from -6 to 6
- out_grad: bfloat16 [8, 512, 256], P('dp'), may hold values from -6 to 6
- weights: bfloat16 [4, 27, 256, 256], P('section'), may hold values from -0.078125 to 0.078125
Outputs:
- level_grads: float32 [4, 8, 512, 256], P('section', 'dp')
- weight_grads: float32 [4, 6912, 256], P('section', 'dp')
The draws below stay inside these ranges and needn't reach their ends.
All inputs are finite; a program needn't handle non-finite values.
Results may differ from the reference program's by a relative error of at most 0.004.
Values sent between devices are 32-bit elements; how exact they have to be, the bound alone decides.
A program may use at most 128 MiB of HBM per device.

```python
import jax
import jax.numpy as jnp
from jax import lax

C = 256
E = 8
VOX = 512
CROPS = 8
LEVELS = 4


def block_levels(stream_key, dims, split, low, largest):
    loudness = 1.0
    for dim, shards_of in split:
        steps = jax.random.uniform(jax.random.fold_in(jax.random.fold_in(stream_key, 6), dim), (shards_of,), jnp.float32, low / len(split), largest / len(split))
        loudness = loudness * jnp.repeat(jnp.exp(steps), dims[dim] // shards_of).reshape((-1,) + (1,) * (len(dims) - 1 - dim))
    return loudness


def bell_draw(key, extent, width, most, cuts=(), kind=jnp.bfloat16):
    result = jax.random.normal(key, extent, jnp.float32) * width
    if len(cuts) > 0:
        result = block_levels(key, extent, cuts, -0.22, 0.18) * result
    return jnp.clip(result, min=-most, max=most).astype(kind)


def setup_inputs(seed: int = 0) -> dict:
    keys = jax.random.split(jax.random.key(seed), 4)
    acts = bell_draw(keys[0], (LEVELS, CROPS, VOX, C), 1.0, 6.0, ((0, 4), (1, 8)))
    out_grad = bell_draw(keys[1], (CROPS, VOX, C), 1.0, 6.0, ((0, 8),))
    weights = bell_draw(keys[2], (LEVELS, 27, C, C), (27 * C) ** -0.5, 0.078125, ((0, 4),))
    return dict(acts=acts, out_grad=out_grad, weights=weights)


def tap_columns(vol, side, flip):
    chans = vol.shape[-1]
    cube = jnp.pad(vol.reshape(side, side, side, chans), ((1, 1), (1, 1), (1, 1), (0, 0)))
    pieces = []
    for first in range(3):
        for second in range(3):
            for third in range(3):
                if flip:
                    aa, bb, cc = 2 - first, 2 - second, 2 - third
                else:
                    aa, bb, cc = first, second, third
                pieces.append(cube[aa:aa + side, bb:bb + side, cc:cc + side].reshape(side ** 3, chans))
    return jnp.concatenate(pieces, axis=1)


def level_back(x_in, grad_in, kernel):
    xf = x_in.astype(jnp.float32)
    hidden = jax.nn.silu(xf).astype(jnp.bfloat16)
    cols = tap_columns(hidden, E, False)
    kernel_grad = jnp.dot(cols.T, grad_in.astype(jnp.bfloat16), preferred_element_type=jnp.float32)
    rcols = tap_columns(grad_in, E, True).reshape(-1, 27, grad_in.shape[-1])
    back = lax.dot_general(rcols, kernel.astype(jnp.float32), (((1, 2), (0, 2)), ((), ())), precision=lax.Precision.HIGHEST)
    sig = jax.nn.sigmoid(xf)
    dsilu = sig * (1.0 + xf * (1.0 - sig))
    out = grad_in + dsilu * back
    return out, kernel_grad


def reference(acts, out_grad, weights):
    levels = weights.shape[0]
    chans = weights.shape[2]

    def crop_step(total, inputs):
        x_all, grad = inputs
        grad = grad.astype(jnp.float32)
        outs = [None] * levels
        for level_index in range(levels - 1, -1, -1):
            grad, kernel_grad = level_back(x_all[level_index], grad, weights[level_index])
            total = total.at[level_index].add(kernel_grad)
            outs[level_index] = grad
        return total, jnp.stack(outs)

    start = jnp.zeros((levels, 27 * chans, chans), jnp.float32)
    total, grads = lax.scan(crop_step, start, (jnp.swapaxes(acts, 0, 1), out_grad))
    level_grads = jnp.swapaxes(grads, 0, 1)
    return level_grads, total * (1.0 / out_grad.shape[0])
```

```python
import functools

import jax
import jax.numpy as jnp
from jax import lax
from jax.experimental import pallas as pl
from jax.experimental.pallas import tpu as pltpu
from jax.sharding import PartitionSpec as P

E = 8
TAPS = 27
PLANE = E * E
GROUP = 4
MESH = pl.DeviceIdType.MESH


def shifted_copies(g_ref, slot, wide):
    chans = g_ref.shape[-1]

    def plane(a, carry):
        rows = pl.ds(pl.multiple_of(a * PLANE, PLANE), PLANE)
        g = g_ref[slot, rows, :].reshape(E, E, chans)
        cell = lax.broadcasted_iota(jnp.int32, (E, E, chans), 1)
        blank = jnp.zeros((1, E, chans), jnp.float32)
        out_rows = pl.ds(pl.multiple_of(a * PLANE + PLANE, PLANE), PLANE)
        for cc in range(3):
            if cc == 0:
                moved = jnp.where(cell == E - 1, 0.0, pltpu.roll(g, E - 1, 1))
            elif cc == 2:
                moved = jnp.where(cell == 0, 0.0, pltpu.roll(g, 1, 1))
            else:
                moved = g
            for bb in range(3):
                if bb == 0:
                    cube = jnp.concatenate([moved[1:], blank], axis=0)
                elif bb == 2:
                    cube = jnp.concatenate([blank, moved[:-1]], axis=0)
                else:
                    cube = moved
                column = (bb * 3 + cc) * chans
                wide[out_rows, column : column + chans] = cube.reshape(PLANE, chans).astype(jnp.bfloat16)
        return carry

    lax.fori_loop(0, E, plane, 0)


def kernel(
    n, levels, rows, span,
    acts, out_grad, weights, level_out, shard_out,
    wcat, hbuf, gbuf, wide, hbf, slope, parts, rbuf,
    w_sem, h_send, h_recv, g_send, g_recv, c_send, c_recv, p_send, p_recv,
):
    groups = n // GROUP
    vox, chans = acts.shape[-2:]
    me = lax.axis_index("dp")
    level = lax.axis_index("section")
    mine = lax.rem(me, GROUP)
    group = me // GROUP
    base = group * GROUP

    barrier = pltpu.get_barrier_semaphore()
    for k in range(1, GROUP):
        pl.semaphore_signal(barrier, inc=1, device_id={"dp": base + lax.rem(mine + k, GROUP)}, device_id_type=MESH)
    for j in range(1, groups):
        pl.semaphore_signal(
            barrier, inc=1, device_id={"dp": lax.rem(group + j, groups) * GROUP + mine}, device_id_type=MESH
        )
    for step in (1, levels - 1):
        pl.semaphore_signal(barrier, inc=1, device_id={"section": lax.rem(level + step, levels)}, device_id_type=MESH)

    def weight_copy(o):
        return pltpu.make_async_copy(
            weights.at[0, o], wcat.at[:, o * chans : (o + 1) * chans], w_sem.at[o]
        )

    for o in range(TAPS):
        weight_copy(o).start()

    @pl.when(level == levels - 1)
    def _():
        gbuf[mine] = out_grad[0].astype(jnp.float32)

    x = acts[0, 0].astype(jnp.float32)
    sig = 1.0 / (1.0 + jnp.exp(-x))
    hidden = (x * sig).astype(jnp.bfloat16).astype(jnp.float32)
    hbuf[mine] = hidden.T
    slope[...] = sig * (1.0 + x * (1.0 - sig))
    edge = jnp.zeros((PLANE, wide.shape[1]), jnp.bfloat16)
    wide[:PLANE, :] = edge
    wide[PLANE + vox :, :] = edge

    pl.semaphore_wait(barrier, GROUP - 1 + groups - 1 + 2)

    def exchange(buf, slot, send, recv, peer):
        return pltpu.make_async_remote_copy(
            src_ref=buf.at[slot], dst_ref=buf.at[slot],
            send_sem=send.at[peer], recv_sem=recv.at[slot],
            device_id={"dp": base + peer}, device_id_type=MESH,
        )

    def peers():
        return [lax.rem(mine + k, GROUP) for k in range(1, GROUP)]

    def chain():
        return pltpu.make_async_remote_copy(
            src_ref=level_out.at[0, 0], dst_ref=gbuf.at[mine],
            send_sem=c_send, recv_sem=c_recv,
            device_id={"section": lax.rem(level + levels - 1, levels)}, device_id_type=MESH,
        )

    for peer in peers():
        exchange(hbuf, mine, h_send, h_recv, peer).start()

    @pl.when(level < levels - 1)
    def _():
        chain().wait_recv()

    for peer in peers():
        exchange(gbuf, mine, g_send, g_recv, peer).start()

    shifted_copies(gbuf, mine, wide)
    for o in range(TAPS):
        weight_copy(o).wait()
    span9 = 9 * chans
    total = None
    for a in range(3):
        term = lax.dot_general(
            wide[(2 - a) * PLANE : (2 - a) * PLANE + vox, :], wcat[:, a * span9 : (a + 1) * span9],
            (((1,), (1,)), ((), ())), preferred_element_type=jnp.float32,
        )
        total = term if total is None else total + term
    level_out[0, 0] = gbuf[mine] + slope[...] * total

    @pl.when(level > 0)
    def _():
        chain().start()

    def owner(j):
        return lax.rem(group + j, groups) * GROUP + mine

    def first_tap(j):
        return owner(j) * rows // chans

    def lead(j):
        return pl.multiple_of(lax.rem(owner(j) * rows, chans), 8)

    def handover(j):
        return pltpu.make_async_remote_copy(
            src_ref=parts.at[j, pl.ds(lead(j), rows)], dst_ref=rbuf.at[j - 1],
            send_sem=p_send.at[j - 1], recv_sem=p_recv.at[j - 1],
            device_id={"dp": owner(j)}, device_id_type=MESH,
        )

    for k in range(GROUP):
        slot = lax.rem(mine + k, GROUP)
        if k > 0:
            exchange(hbuf, slot, h_send, h_recv, slot).wait_recv()
            exchange(gbuf, slot, g_send, g_recv, slot).wait_recv()
            shifted_copies(gbuf, slot, wide)
        hbf[...] = hbuf[slot].astype(jnp.bfloat16)
        for j in list(range(1, groups)) + [0]:
            start = first_tap(j)

            def tap_step(i, carry):
                tap = jnp.minimum(start + i, TAPS - 1)
                plane = pl.ds(pl.multiple_of((2 - tap // 9) * PLANE, PLANE), vox)
                column = pl.ds(pl.multiple_of(lax.rem(tap, 9) * chans, chans), chans)
                place = pl.ds(pl.multiple_of(i * chans, chans), chans)
                term = jnp.dot(hbf[...], wide[plane, column], preferred_element_type=jnp.float32)
                if k == 0:
                    parts[j, place, :] = term
                else:
                    parts[j, place, :] += term
                return carry

            lax.fori_loop(0, span, tap_step, 0)
            if k == GROUP - 1 and j > 0:
                handover(j).start()

    result = parts[0, pl.ds(lead(0), rows), :]
    for j in range(1, groups):
        handover(j).wait_recv()
        result = result + rbuf[j - 1]
    shard_out[0] = result * (1.0 / n)

    for peer in peers():
        exchange(hbuf, mine, h_send, h_recv, peer).wait_send()
        exchange(gbuf, mine, g_send, g_recv, peer).wait_send()
    for j in range(1, groups):
        handover(j).wait_send()

    @pl.when(level > 0)
    def _():
        chain().wait_send()


def body(acts, out_grad, weights):
    n = lax.axis_size("dp")
    levels = lax.axis_size("section")
    vox, chans = acts.shape[2:]
    rows = TAPS * chans // n
    groups = n // GROUP
    span = max((d * rows + rows - 1) // chans - d * rows // chans + 1 for d in range(n))
    sems = pltpu.SemaphoreType.DMA
    return pl.pallas_call(
        functools.partial(kernel, n, levels, rows, span),
        out_shape=(
            jax.ShapeDtypeStruct(acts.shape, jnp.float32),
            jax.ShapeDtypeStruct((1, rows, chans), jnp.float32),
        ),
        in_specs=[
            pl.BlockSpec(memory_space=pltpu.VMEM),
            pl.BlockSpec(memory_space=pltpu.VMEM),
            pl.BlockSpec(memory_space=pl.ANY),
        ],
        out_specs=(pl.BlockSpec(memory_space=pltpu.VMEM), pl.BlockSpec(memory_space=pltpu.VMEM)),
        scratch_shapes=[
            pltpu.VMEM((chans, TAPS * chans), jnp.bfloat16),
            pltpu.VMEM((GROUP, chans, vox), jnp.float32),
            pltpu.VMEM((GROUP, vox, chans), jnp.float32),
            pltpu.VMEM((vox + 2 * PLANE, 9 * chans), jnp.bfloat16),
            pltpu.VMEM((chans, vox), jnp.bfloat16),
            pltpu.VMEM((vox, chans), jnp.float32),
            pltpu.VMEM((groups, span * chans, chans), jnp.float32),
            pltpu.VMEM((max(groups - 1, 1), rows, chans), jnp.float32),
            sems((TAPS,)),
            sems((GROUP,)), sems((GROUP,)), sems((GROUP,)), sems((GROUP,)),
            sems, sems,
            sems((max(groups - 1, 1),)), sems((max(groups - 1, 1),)),
        ],
        compiler_params=pltpu.CompilerParams(
            collective_id=0, has_side_effects=True, vmem_limit_bytes=50 * 1024 * 1024
        ),
        cost_estimate=pl.CostEstimate(flops=4 * 10**9, bytes_accessed=6 * 10**6, transcendentals=vox * chans),
    )(acts, out_grad, weights)


def solution(mesh):
    return jax.shard_map(
        body,
        mesh=mesh,
        in_specs=(
            P("section", "dp", None, None),
            P("dp", None, None),
            P("section", None, None, None),
        ),
        out_specs=(P("section", "dp", None, None), P("section", "dp", None)),
        check_vma=False,
    )
```

```python
import functools

import jax
import jax.numpy as jnp
from jax import lax
from jax.experimental import pallas as pl
from jax.experimental.pallas import tpu as pltpu
from jax.sharding import PartitionSpec as P

E = 8
TAPS = 27
PLANE = E * E
GROUP = 4
MESH = pl.DeviceIdType.MESH


def shifted_copies(plane_of, chans, wide):
    def plane(a, carry):
        rows = pl.ds(pl.multiple_of(a * PLANE, PLANE), PLANE)
        g = plane_of(rows).reshape(E, E, chans)
        cell = lax.broadcasted_iota(jnp.int32, (E, E, chans), 1)
        blank = jnp.zeros((1, E, chans), jnp.float32)
        out_rows = pl.ds(pl.multiple_of(a * PLANE + PLANE, PLANE), PLANE)
        for cc in range(3):
            if cc == 0:
                moved = jnp.where(cell == E - 1, 0.0, pltpu.roll(g, E - 1, 1))
            elif cc == 2:
                moved = jnp.where(cell == 0, 0.0, pltpu.roll(g, 1, 1))
            else:
                moved = g
            for bb in range(3):
                if bb == 0:
                    cube = jnp.concatenate([moved[1:], blank], axis=0)
                elif bb == 2:
                    cube = jnp.concatenate([blank, moved[:-1]], axis=0)
                else:
                    cube = moved
                column = (bb * 3 + cc) * chans
                wide[out_rows, column : column + chans] = cube.reshape(PLANE, chans).astype(jnp.bfloat16)
        return carry

    lax.fori_loop(0, E, plane, 0)


def kernel(
    n, levels, rows, span, reach,
    acts, out_grad, weights, level_out, shard_out,
    wcat, hown, hin, gown, gin, wide, narrow, slope, parts, rbuf, done, final,
    w_sem, h_send, h_recv, g_send, g_recv, c_send, c_recv, p_send, p_recv, f_send, f_recv,
):
    groups = n // GROUP
    vox, chans = acts.shape[-2:]
    half = chans // 2
    me = lax.axis_index("dp")
    level = lax.axis_index("section")
    mine = lax.rem(me, GROUP)
    group = me // GROUP
    base = group * GROUP

    barrier = pltpu.get_barrier_semaphore()
    for k in range(1, GROUP):
        pl.semaphore_signal(barrier, inc=1, device_id={"dp": base + lax.rem(mine + k, GROUP)}, device_id_type=MESH)
    for j in range(1, groups):
        pl.semaphore_signal(
            barrier, inc=1, device_id={"dp": lax.rem(group + j, groups) * GROUP + mine}, device_id_type=MESH
        )
    for step in (1, levels - 1):
        pl.semaphore_signal(barrier, inc=1, device_id={"section": lax.rem(level + step, levels)}, device_id_type=MESH)

    def weight_copy(o):
        return pltpu.make_async_copy(
            weights.at[0, o], wcat.at[:, o * chans : (o + 1) * chans], w_sem.at[o]
        )

    for o in range(TAPS):
        weight_copy(o).start()

    @pl.when(level == levels - 1)
    def _():
        gown[...] = out_grad[0].astype(jnp.float32)

    x = acts[0, 0].astype(jnp.float32)
    sig = 1.0 / (1.0 + jnp.exp(-x))
    hidden = (x * sig).astype(jnp.bfloat16).astype(jnp.float32)
    hown[...] = hidden.T

    def row_half(place):
        return pl.ds(pl.multiple_of(lax.rem(place, 2) * half, half), half)

    def column_half(place):
        return pl.ds(pl.multiple_of(place // 2 * half, half), half)

    def send_hidden(peer):
        return pltpu.make_async_remote_copy(
            src_ref=hown.at[row_half(peer)], dst_ref=hin.at[mine],
            send_sem=h_send.at[peer], recv_sem=h_recv.at[mine],
            device_id={"dp": base + peer}, device_id_type=MESH,
        )

    def send_cotangent(peer):
        return pltpu.make_async_remote_copy(
            src_ref=gown.at[:, column_half(peer)], dst_ref=gin.at[mine],
            send_sem=g_send.at[peer], recv_sem=g_recv.at[mine],
            device_id={"dp": base + peer}, device_id_type=MESH,
        )

    def arrived(buf, slot, send, recv):
        pltpu.make_async_remote_copy(
            src_ref=buf.at[slot], dst_ref=buf.at[slot],
            send_sem=send.at[slot], recv_sem=recv.at[slot],
            device_id={"dp": base + slot}, device_id_type=MESH,
        ).wait_recv()

    def chain():
        return pltpu.make_async_remote_copy(
            src_ref=level_out.at[0, 0], dst_ref=gown,
            send_sem=c_send, recv_sem=c_recv,
            device_id={"section": lax.rem(level + levels - 1, levels)}, device_id_type=MESH,
        )

    peers = [lax.rem(mine + k, GROUP) for k in range(1, GROUP)]

    pl.semaphore_wait(barrier, GROUP - 1 + groups - 1 + 2)
    for peer in peers:
        send_hidden(peer).start()

    slope[...] = sig * (1.0 + x * (1.0 - sig))
    for buf in (wide, narrow):
        edge = jnp.zeros((PLANE, buf.shape[1]), jnp.bfloat16)
        buf[:PLANE, :] = edge
        buf[PLANE + vox :, :] = edge

    @pl.when(level < levels - 1)
    def _():
        chain().wait_recv()

    for peer in peers:
        send_cotangent(peer).start()

    shifted_copies(lambda at: gown[at, :], chans, wide)
    for o in range(TAPS):
        weight_copy(o).wait()
    nine = 9 * chans
    total = None
    for a in range(3):
        term = lax.dot_general(
            wide[(2 - a) * PLANE : (2 - a) * PLANE + vox, :], wcat[:, a * nine : (a + 1) * nine],
            (((1,), (1,)), ((), ())), preferred_element_type=jnp.float32,
        )
        total = term if total is None else total + term
    level_out[0, 0] = gown[...] + slope[...] * total

    @pl.when(level > 0)
    def _():
        chain().start()

    def overlaps(place, tap, first, count):
        low = tap * chans + lax.rem(place, 2) * half
        return (low < (first + count) * rows) & (low + half > first * rows)

    def group_tap(g):
        return g * GROUP * rows // chans

    def handover(j, tap):
        to = lax.rem(group + j, groups)
        at = tap - group_tap(to)
        return pltpu.make_async_remote_copy(
            src_ref=parts.at[tap], dst_ref=rbuf.at[j - 1, at],
            send_sem=p_send.at[j - 1, at], recv_sem=p_recv.at[j - 1, at],
            device_id={"dp": to * GROUP + mine}, device_id_type=MESH,
        )

    def needed(j, tap):
        return overlaps(mine, tap, lax.rem(group + j, groups) * GROUP, GROUP)

    leading = group_tap(lax.rem(group + 1, groups)) // 9
    for k in range(GROUP):
        slot = lax.rem(mine + k, GROUP)
        if k == 0:
            left = hown[row_half(mine), :].astype(jnp.bfloat16)
            shifted_copies(lambda at: gown[at, column_half(mine)], half, narrow)
        else:
            arrived(hin, slot, h_send, h_recv)
            left = hin[slot].astype(jnp.bfloat16)
            arrived(gin, slot, g_send, g_recv)
            shifted_copies(lambda at: gin[slot, at, :], half, narrow)
        for step in range(3):
            a = lax.rem(leading + step, 3)
            at = pl.ds(pl.multiple_of((2 - a) * PLANE, PLANE), vox)
            term = jnp.dot(left, narrow[at, :], preferred_element_type=jnp.float32)
            for bc in range(9):
                piece = term[:, bc * half : (bc + 1) * half]
                if k == 0:
                    parts[a * 9 + bc] = piece
                else:
                    parts[a * 9 + bc] += piece
            if k == GROUP - 1:

                def hand_on(bc, carry):
                    tap = a * 9 + bc
                    for j in range(1, groups):

                        @pl.when(needed(j, tap))
                        def _():
                            handover(j, tap).start()

                    return carry

                lax.fori_loop(0, 9, hand_on, 0)

    def owner_tap(place):
        return (base + place) * rows // chans

    def deliver(u, tap, peer):
        at = tap - owner_tap(peer)
        return pltpu.make_async_remote_copy(
            src_ref=done.at[u],
            dst_ref=final.at[pl.ds(pl.multiple_of(at * chans + lax.rem(mine, 2) * half, half), half), column_half(mine)],
            send_sem=f_send.at[peer, at], recv_sem=f_recv.at[mine, at],
            device_id={"dp": base + peer}, device_id_type=MESH,
        )

    def finish(u, carry):
        tap = group_tap(group) + u

        @pl.when(overlaps(mine, tap, base, GROUP))
        def _():
            value = parts[tap]
            for j in range(1, groups):
                pltpu.make_async_remote_copy(
                    src_ref=parts.at[tap], dst_ref=rbuf.at[j - 1, u],
                    send_sem=p_send.at[j - 1, u], recv_sem=p_recv.at[j - 1, u],
                    device_id={"dp": lax.rem(group + j, groups) * GROUP + mine}, device_id_type=MESH,
                ).wait_recv()
                value = value + rbuf[j - 1, u]
            value = value * (1.0 / n)
            done[u] = value
            for peer in peers:

                @pl.when(overlaps(mine, tap, base + peer, 1))
                def _():
                    deliver(u, tap, peer).start()

            @pl.when(overlaps(mine, tap, me, 1))
            def _():
                at = (tap - owner_tap(mine)) * chans + lax.rem(mine, 2) * half
                final[pl.ds(pl.multiple_of(at, half), half), column_half(mine)] = value

        return carry

    lax.fori_loop(0, reach, finish, 0)

    def collect(at, carry):
        tap = owner_tap(mine) + at
        for peer in peers:

            @pl.when(overlaps(peer, tap, me, 1))
            def _():
                pltpu.make_async_remote_copy(
                    src_ref=done.at[0],
                    dst_ref=final.at[
                        pl.ds(pl.multiple_of(at * chans + lax.rem(peer, 2) * half, half), half), column_half(peer)
                    ],
                    send_sem=f_send.at[peer, at], recv_sem=f_recv.at[peer, at],
                    device_id={"dp": base + peer}, device_id_type=MESH,
                ).wait_recv()

        return carry

    lax.fori_loop(0, span, collect, 0)
    shard_out[0] = final[pl.ds(pl.multiple_of(lax.rem(me * rows, chans), 8), rows), :]

    for peer in peers:
        send_hidden(peer).wait_send()
        send_cotangent(peer).wait_send()

    def drain(tap, carry):
        for j in range(1, groups):

            @pl.when(needed(j, tap))
            def _():
                handover(j, tap).wait_send()

        for peer in peers:

            @pl.when(overlaps(mine, tap, base + peer, 1))
            def _():
                deliver(tap - group_tap(group), tap, peer).wait_send()

        return carry

    lax.fori_loop(0, TAPS, drain, 0)

    @pl.when(level > 0)
    def _():
        chain().wait_send()


def body(acts, out_grad, weights):
    n = lax.axis_size("dp")
    levels = lax.axis_size("section")
    vox, chans = acts.shape[2:]
    half = chans // 2
    rows = TAPS * chans // n
    groups = n // GROUP
    others = max(groups - 1, 1)

    def most(width):
        return max((d + width - 1) // chans - d // chans + 1 for d in range(0, TAPS * chans, width))

    span, reach = most(rows), most(rows * GROUP)
    sems = pltpu.SemaphoreType.DMA
    f32, b16 = jnp.float32, jnp.bfloat16
    return pl.pallas_call(
        functools.partial(kernel, n, levels, rows, span, reach),
        out_shape=(
            jax.ShapeDtypeStruct(acts.shape, f32),
            jax.ShapeDtypeStruct((1, rows, chans), f32),
        ),
        in_specs=[
            pl.BlockSpec(memory_space=pltpu.VMEM),
            pl.BlockSpec(memory_space=pltpu.VMEM),
            pl.BlockSpec(memory_space=pl.ANY),
        ],
        out_specs=(pl.BlockSpec(memory_space=pltpu.VMEM), pl.BlockSpec(memory_space=pltpu.VMEM)),
        scratch_shapes=[
            pltpu.VMEM((chans, TAPS * chans), b16),
            pltpu.VMEM((chans, vox), f32),
            pltpu.VMEM((GROUP, half, vox), f32),
            pltpu.VMEM((vox, chans), f32),
            pltpu.VMEM((GROUP, vox, half), f32),
            pltpu.VMEM((vox + 2 * PLANE, 9 * chans), b16),
            pltpu.VMEM((vox + 2 * PLANE, 9 * half), b16),
            pltpu.VMEM((vox, chans), f32),
            pltpu.VMEM((TAPS, half, half), f32),
            pltpu.VMEM((others, reach, half, half), f32),
            pltpu.VMEM((reach, half, half), f32),
            pltpu.VMEM((span * chans, chans), f32),
            sems((TAPS,)),
            sems((GROUP,)), sems((GROUP,)), sems((GROUP,)), sems((GROUP,)),
            sems, sems,
            sems((others, reach)), sems((others, reach)),
            sems((GROUP, span)), sems((GROUP, span)),
        ],
        compiler_params=pltpu.CompilerParams(
            collective_id=0, has_side_effects=True, vmem_limit_bytes=50 * 1024 * 1024
        ),
        cost_estimate=pl.CostEstimate(flops=4 * 10**9, bytes_accessed=6 * 10**6, transcendentals=vox * chans),
    )(acts, out_grad, weights)


def solution(mesh):
    return jax.shard_map(
        body,
        mesh=mesh,
        in_specs=(
            P("section", "dp", None, None),
            P("dp", None, None),
            P("section", None, None, None),
        ),
        out_specs=(P("section", "dp", None, None), P("section", "dp", None)),
        check_vma=False,
    )
```

```python
import functools

import jax
import jax.numpy as jnp
from jax import lax
from jax.experimental import pallas as pl
from jax.experimental.pallas import tpu as pltpu
from jax.sharding import PartitionSpec as P

E = 8
TAPS = 27
PLANE = E * E
GROUP = 4
MESH = pl.DeviceIdType.MESH


def shifted_copies(plane_of, chans, wide):
    def plane(a, carry):
        rows = pl.ds(pl.multiple_of(a * PLANE, PLANE), PLANE)
        g = plane_of(rows).reshape(E, E, chans)
        cell = lax.broadcasted_iota(jnp.int32, (E, E, chans), 1)
        blank = jnp.zeros((1, E, chans), jnp.float32)
        for cc in range(3):
            if cc == 0:
                moved = jnp.where(cell == E - 1, 0.0, pltpu.roll(g, E - 1, 1))
            elif cc == 2:
                moved = jnp.where(cell == 0, 0.0, pltpu.roll(g, 1, 1))
            else:
                moved = g
            for bb in range(3):
                if bb == 0:
                    cube = jnp.concatenate([moved[1:], blank], axis=0)
                elif bb == 2:
                    cube = jnp.concatenate([blank, moved[:-1]], axis=0)
                else:
                    cube = moved
                column = (bb * 3 + cc) * chans
                wide[rows, column : column + chans] = cube.reshape(PLANE, chans).astype(jnp.bfloat16)
        return carry

    lax.fori_loop(0, E, plane, 0)


def kernel(
    n, levels, rows, span, reach,
    acts, out_grad, weights, level_out, shard_out,
    wcat, hown, hin, gown, gin, wide, narrow, slope, parts, rbuf, done, final,
    w_sem, h_send, h_recv, g_send, g_recv, c_send, c_recv, p_send, p_recv, f_send, f_recv,
):
    groups = n // GROUP
    vox, chans = acts.shape[-2:]
    half = chans // 2
    me = lax.axis_index("dp")
    level = lax.axis_index("section")
    mine = lax.rem(me, GROUP)
    group = me // GROUP
    base = group * GROUP

    barrier = pltpu.get_barrier_semaphore()
    for k in range(1, GROUP):
        pl.semaphore_signal(barrier, inc=1, device_id={"dp": base + lax.rem(mine + k, GROUP)}, device_id_type=MESH)
    for j in range(1, groups):
        pl.semaphore_signal(
            barrier, inc=1, device_id={"dp": lax.rem(group + j, groups) * GROUP + mine}, device_id_type=MESH
        )
    for step in (1, levels - 1):
        pl.semaphore_signal(barrier, inc=1, device_id={"section": lax.rem(level + step, levels)}, device_id_type=MESH)

    def weight_copy(o):
        return pltpu.make_async_copy(
            weights.at[0, o],
            wcat.at[o // 9 * chans : (o // 9 + 1) * chans, o % 9 * chans : (o % 9 + 1) * chans],
            w_sem.at[o],
        )

    for o in range(TAPS):
        weight_copy(o).start()

    @pl.when(level == levels - 1)
    def _():
        gown[...] = out_grad[0].astype(jnp.float32)

    x = acts[0, 0].astype(jnp.float32)
    sig = 1.0 / (1.0 + jnp.exp(-x))
    hidden = (x * sig).astype(jnp.bfloat16).astype(jnp.float32)
    hown[...] = hidden.T

    def row_half(place):
        return pl.ds(pl.multiple_of(lax.rem(place, 2) * half, half), half)

    def column_half(place):
        return pl.ds(pl.multiple_of(place // 2 * half, half), half)

    def send_hidden(peer):
        return pltpu.make_async_remote_copy(
            src_ref=hown.at[row_half(peer)], dst_ref=hin.at[mine],
            send_sem=h_send.at[peer], recv_sem=h_recv.at[mine],
            device_id={"dp": base + peer}, device_id_type=MESH,
        )

    def send_cotangent(peer):
        return pltpu.make_async_remote_copy(
            src_ref=gown.at[:, column_half(peer)], dst_ref=gin.at[mine],
            send_sem=g_send.at[peer], recv_sem=g_recv.at[mine],
            device_id={"dp": base + peer}, device_id_type=MESH,
        )

    def arrived(buf, slot, send, recv):
        pltpu.make_async_remote_copy(
            src_ref=buf.at[slot], dst_ref=buf.at[slot],
            send_sem=send.at[slot], recv_sem=recv.at[slot],
            device_id={"dp": base + slot}, device_id_type=MESH,
        ).wait_recv()

    def chain():
        return pltpu.make_async_remote_copy(
            src_ref=level_out.at[0, 0], dst_ref=gown,
            send_sem=c_send, recv_sem=c_recv,
            device_id={"section": lax.rem(level + levels - 1, levels)}, device_id_type=MESH,
        )

    peers = [lax.rem(mine + k, GROUP) for k in range(1, GROUP)]

    pl.semaphore_wait(barrier, GROUP - 1 + groups - 1 + 2)
    for peer in peers:
        send_hidden(peer).start()

    slope[...] = sig * (1.0 + x * (1.0 - sig))

    @pl.when(level < levels - 1)
    def _():
        chain().wait_recv()

    for peer in peers:
        send_cotangent(peer).start()

    shifted_copies(lambda at: gown[at, :], chans, wide)
    for o in range(TAPS):
        weight_copy(o).wait()
    planes = lax.dot_general(
        wide[...], wcat[...], (((1,), (1,)), ((), ())), preferred_element_type=jnp.float32
    )
    edge = jnp.zeros((PLANE, chans), jnp.float32)
    total = (
        planes[:, chans : 2 * chans]
        + jnp.concatenate([planes[PLANE:, :chans], edge], axis=0)
        + jnp.concatenate([edge, planes[: vox - PLANE, 2 * chans :]], axis=0)
    )
    level_out[0, 0] = gown[...] + slope[...] * total

    @pl.when(level > 0)
    def _():
        chain().start()

    def overlaps(place, tap, first, count):
        low = tap * chans + lax.rem(place, 2) * half
        return (low < (first + count) * rows) & (low + half > first * rows)

    def group_tap(g):
        return g * GROUP * rows // chans

    def handover(j, tap):
        to = lax.rem(group + j, groups)
        at = tap - group_tap(to)
        return pltpu.make_async_remote_copy(
            src_ref=parts.at[tap], dst_ref=rbuf.at[j - 1, at],
            send_sem=p_send.at[j - 1, at], recv_sem=p_recv.at[j - 1, at],
            device_id={"dp": to * GROUP + mine}, device_id_type=MESH,
        )

    def needed(j, tap):
        return overlaps(mine, tap, lax.rem(group + j, groups) * GROUP, GROUP)

    leading = group_tap(lax.rem(group + 1, groups))
    for k in range(GROUP):
        slot = lax.rem(mine + k, GROUP)
        if k == 0:
            h = hown[row_half(mine), :]
            shifted_copies(lambda at: gown[at, column_half(mine)], half, narrow)
        else:
            arrived(hin, slot, h_send, h_recv)
            h = hin[slot]
            arrived(gin, slot, g_send, g_recv)
            shifted_copies(lambda at: gin[slot, at, :], half, narrow)
        cell = lax.broadcasted_iota(jnp.int32, (half, vox), 1)
        above = jnp.where(cell < PLANE, 0.0, pltpu.roll(h, PLANE, 1))
        below = jnp.where(cell >= vox - PLANE, 0.0, pltpu.roll(h, vox - PLANE, 1))
        left = jnp.concatenate([above, h, below], axis=0).astype(jnp.bfloat16)
        term = jnp.dot(left, narrow[...], preferred_element_type=jnp.float32)
        for tap in range(TAPS):
            a, bc = divmod(tap, 9)
            piece = term[a * half : (a + 1) * half, bc * half : (bc + 1) * half]
            if k == 0:
                parts[tap] = piece
            else:
                parts[tap] += piece
        if k == GROUP - 1:

            def hand_on(i, carry):
                tap = lax.rem(leading + i, TAPS)
                for j in range(1, groups):

                    @pl.when(needed(j, tap))
                    def _():
                        handover(j, tap).start()

                return carry

            lax.fori_loop(0, TAPS, hand_on, 0)

    def owner_tap(place):
        return (base + place) * rows // chans

    def deliver(u, tap, peer):
        at = tap - owner_tap(peer)
        return pltpu.make_async_remote_copy(
            src_ref=done.at[u],
            dst_ref=final.at[pl.ds(pl.multiple_of(at * chans + lax.rem(mine, 2) * half, half), half), column_half(mine)],
            send_sem=f_send.at[peer, at], recv_sem=f_recv.at[mine, at],
            device_id={"dp": base + peer}, device_id_type=MESH,
        )

    def finish(u, carry):
        tap = group_tap(group) + u

        @pl.when(overlaps(mine, tap, base, GROUP))
        def _():
            value = parts[tap]
            for j in range(1, groups):
                pltpu.make_async_remote_copy(
                    src_ref=parts.at[tap], dst_ref=rbuf.at[j - 1, u],
                    send_sem=p_send.at[j - 1, u], recv_sem=p_recv.at[j - 1, u],
                    device_id={"dp": lax.rem(group + j, groups) * GROUP + mine}, device_id_type=MESH,
                ).wait_recv()
                value = value + rbuf[j - 1, u]
            value = value * (1.0 / n)
            done[u] = value
            for peer in peers:

                @pl.when(overlaps(mine, tap, base + peer, 1))
                def _():
                    deliver(u, tap, peer).start()

            @pl.when(overlaps(mine, tap, me, 1))
            def _():
                at = (tap - owner_tap(mine)) * chans + lax.rem(mine, 2) * half
                final[pl.ds(pl.multiple_of(at, half), half), column_half(mine)] = value

        return carry

    lax.fori_loop(0, reach, finish, 0)

    def collect(at, carry):
        tap = owner_tap(mine) + at
        for peer in peers:

            @pl.when(overlaps(peer, tap, me, 1))
            def _():
                pltpu.make_async_remote_copy(
                    src_ref=done.at[0],
                    dst_ref=final.at[
                        pl.ds(pl.multiple_of(at * chans + lax.rem(peer, 2) * half, half), half), column_half(peer)
                    ],
                    send_sem=f_send.at[peer, at], recv_sem=f_recv.at[peer, at],
                    device_id={"dp": base + peer}, device_id_type=MESH,
                ).wait_recv()

        return carry

    lax.fori_loop(0, span, collect, 0)
    shard_out[0] = final[pl.ds(pl.multiple_of(lax.rem(me * rows, chans), 8), rows), :]

    for peer in peers:
        send_hidden(peer).wait_send()
        send_cotangent(peer).wait_send()

    def drain(tap, carry):
        for j in range(1, groups):

            @pl.when(needed(j, tap))
            def _():
                handover(j, tap).wait_send()

        for peer in peers:

            @pl.when(overlaps(mine, tap, base + peer, 1))
            def _():
                deliver(tap - group_tap(group), tap, peer).wait_send()

        return carry

    lax.fori_loop(0, TAPS, drain, 0)

    @pl.when(level > 0)
    def _():
        chain().wait_send()


def body(acts, out_grad, weights):
    n = lax.axis_size("dp")
    levels = lax.axis_size("section")
    vox, chans = acts.shape[2:]
    half = chans // 2
    rows = TAPS * chans // n
    groups = n // GROUP
    others = max(groups - 1, 1)

    def most(width):
        return max((d + width - 1) // chans - d // chans + 1 for d in range(0, TAPS * chans, width))

    span, reach = most(rows), most(rows * GROUP)
    sems = pltpu.SemaphoreType.DMA
    f32, b16 = jnp.float32, jnp.bfloat16
    return pl.pallas_call(
        functools.partial(kernel, n, levels, rows, span, reach),
        out_shape=(
            jax.ShapeDtypeStruct(acts.shape, f32),
            jax.ShapeDtypeStruct((1, rows, chans), f32),
        ),
        in_specs=[
            pl.BlockSpec(memory_space=pltpu.VMEM),
            pl.BlockSpec(memory_space=pltpu.VMEM),
            pl.BlockSpec(memory_space=pl.ANY),
        ],
        out_specs=(pl.BlockSpec(memory_space=pltpu.VMEM), pl.BlockSpec(memory_space=pltpu.VMEM)),
        scratch_shapes=[
            pltpu.VMEM((3 * chans, 9 * chans), b16),
            pltpu.VMEM((chans, vox), f32),
            pltpu.VMEM((GROUP, half, vox), f32),
            pltpu.VMEM((vox, chans), f32),
            pltpu.VMEM((GROUP, vox, half), f32),
            pltpu.VMEM((vox, 9 * chans), b16),
            pltpu.VMEM((vox, 9 * half), b16),
            pltpu.VMEM((vox, chans), f32),
            pltpu.VMEM((TAPS, half, half), f32),
            pltpu.VMEM((others, reach, half, half), f32),
            pltpu.VMEM((reach, half, half), f32),
            pltpu.VMEM((span * chans, chans), f32),
            sems((TAPS,)),
            sems((GROUP,)), sems((GROUP,)), sems((GROUP,)), sems((GROUP,)),
            sems, sems,
            sems((others, reach)), sems((others, reach)),
            sems((GROUP, span)), sems((GROUP, span)),
        ],
        compiler_params=pltpu.CompilerParams(
            collective_id=0, has_side_effects=True, vmem_limit_bytes=50 * 1024 * 1024
        ),
        cost_estimate=pl.CostEstimate(flops=4 * 10**9, bytes_accessed=6 * 10**6, transcendentals=vox * chans),
    )(acts, out_grad, weights)


def solution(mesh):
    return jax.shard_map(
        body,
        mesh=mesh,
        in_specs=(
            P("section", "dp", None, None),
            P("dp", None, None),
            P("section", None, None, None),
        ),
        out_specs=(P("section", "dp", None, None), P("section", "dp", None)),
        check_vma=False,
    )
```

```python
import functools

import jax
import jax.numpy as jnp
from jax import lax
from jax.experimental import pallas as pl
from jax.experimental.pallas import tpu as pltpu
from jax.sharding import PartitionSpec as P

E = 8
TAPS = 27
PLANE = E * E
GROUP = 4
MESH = pl.DeviceIdType.MESH


def shifted_copies(plane_of, chans, wide):
    def plane(a, carry):
        rows = pl.ds(pl.multiple_of(a * PLANE, PLANE), PLANE)
        g = plane_of(rows).reshape(E, E, chans)
        cell = lax.broadcasted_iota(jnp.int32, (E, E, chans), 1)
        blank = jnp.zeros((1, E, chans), jnp.float32)
        out_rows = pl.ds(pl.multiple_of(a * PLANE + PLANE, PLANE), PLANE)
        for cc in range(3):
            if cc == 0:
                moved = jnp.where(cell == E - 1, 0.0, pltpu.roll(g, E - 1, 1))
            elif cc == 2:
                moved = jnp.where(cell == 0, 0.0, pltpu.roll(g, 1, 1))
            else:
                moved = g
            for bb in range(3):
                if bb == 0:
                    cube = jnp.concatenate([moved[1:], blank], axis=0)
                elif bb == 2:
                    cube = jnp.concatenate([blank, moved[:-1]], axis=0)
                else:
                    cube = moved
                column = (bb * 3 + cc) * chans
                wide[out_rows, column : column + chans] = cube.reshape(PLANE, chans).astype(jnp.bfloat16)
        return carry

    lax.fori_loop(0, E, plane, 0)


def kernel(
    n, levels, rows, span, reach,
    acts, out_grad, weights, level_out, shard_out,
    wcat, hown, hin, gown, gin, wide, narrow, slope, parts, rbuf, done, final,
    w_sem, h_send, h_recv, g_send, g_recv, c_send, c_recv, p_send, p_recv, f_send, f_recv,
):
    groups = n // GROUP
    vox, chans = acts.shape[-2:]
    half = chans // 2
    me = lax.axis_index("dp")
    level = lax.axis_index("section")
    mine = lax.rem(me, GROUP)
    group = me // GROUP
    base = group * GROUP

    barrier = pltpu.get_barrier_semaphore()
    for k in range(1, GROUP):
        pl.semaphore_signal(barrier, inc=1, device_id={"dp": base + lax.rem(mine + k, GROUP)}, device_id_type=MESH)
    for j in range(1, groups):
        pl.semaphore_signal(
            barrier, inc=1, device_id={"dp": lax.rem(group + j, groups) * GROUP + mine}, device_id_type=MESH
        )
    for step in (1, levels - 1):
        pl.semaphore_signal(barrier, inc=1, device_id={"section": lax.rem(level + step, levels)}, device_id_type=MESH)

    def weight_copy(o):
        return pltpu.make_async_copy(
            weights.at[0, o], wcat.at[:, o * chans : (o + 1) * chans], w_sem.at[o]
        )

    for o in range(TAPS):
        weight_copy(o).start()

    @pl.when(level == levels - 1)
    def _():
        gown[...] = out_grad[0].astype(jnp.float32)

    x = acts[0, 0].astype(jnp.float32)
    sig = 1.0 / (1.0 + jnp.exp(-x))
    hidden = (x * sig).astype(jnp.bfloat16).astype(jnp.float32)
    hown[...] = hidden.T

    def row_half(place):
        return pl.ds(pl.multiple_of(lax.rem(place, 2) * half, half), half)

    def column_half(place):
        return pl.ds(pl.multiple_of(place // 2 * half, half), half)

    def send_hidden(peer):
        return pltpu.make_async_remote_copy(
            src_ref=hown.at[row_half(peer)], dst_ref=hin.at[mine],
            send_sem=h_send.at[peer], recv_sem=h_recv.at[mine],
            device_id={"dp": base + peer}, device_id_type=MESH,
        )

    def send_cotangent(peer):
        return pltpu.make_async_remote_copy(
            src_ref=gown.at[:, column_half(peer)], dst_ref=gin.at[mine],
            send_sem=g_send.at[peer], recv_sem=g_recv.at[mine],
            device_id={"dp": base + peer}, device_id_type=MESH,
        )

    def arrived(buf, slot, send, recv):
        pltpu.make_async_remote_copy(
            src_ref=buf.at[slot], dst_ref=buf.at[slot],
            send_sem=send.at[slot], recv_sem=recv.at[slot],
            device_id={"dp": base + slot}, device_id_type=MESH,
        ).wait_recv()

    def chain():
        return pltpu.make_async_remote_copy(
            src_ref=level_out.at[0, 0], dst_ref=gown,
            send_sem=c_send, recv_sem=c_recv,
            device_id={"section": lax.rem(level + levels - 1, levels)}, device_id_type=MESH,
        )

    peers = [mine + 1 - 2 * lax.rem(mine, 2), lax.rem(mine + 2, GROUP), GROUP - 1 - mine]

    pl.semaphore_wait(barrier, GROUP - 1 + groups - 1 + 2)
    for peer in peers:
        send_hidden(peer).start()

    slope[...] = sig * (1.0 + x * (1.0 - sig))
    for buf in (wide, narrow):
        edge = jnp.zeros((PLANE, buf.shape[1]), jnp.bfloat16)
        buf[:PLANE, :] = edge
        buf[PLANE + vox :, :] = edge

    @pl.when(level < levels - 1)
    def _():
        chain().wait_recv()

    for peer in peers[:2]:
        send_cotangent(peer).start()

    shifted_copies(lambda at: gown[at, :], chans, wide)
    for o in range(TAPS):
        weight_copy(o).wait()
    nine = 9 * chans
    total = None
    for a in range(3):
        term = lax.dot_general(
            wide[(2 - a) * PLANE : (2 - a) * PLANE + vox, :], wcat[:, a * nine : (a + 1) * nine],
            (((1,), (1,)), ((), ())), preferred_element_type=jnp.float32,
        )
        total = term if total is None else total + term
    level_out[0, 0] = gown[...] + slope[...] * total

    @pl.when(level > 0)
    def _():
        chain().start()

    def overlaps(place, tap, first, count):
        low = tap * chans + lax.rem(place, 2) * half
        return (low < (first + count) * rows) & (low + half > first * rows)

    def group_tap(g):
        return g * GROUP * rows // chans

    def handover(j, tap):
        to = lax.rem(group + j, groups)
        at = tap - group_tap(to)
        return pltpu.make_async_remote_copy(
            src_ref=parts.at[tap], dst_ref=rbuf.at[j - 1, at],
            send_sem=p_send.at[j - 1, at], recv_sem=p_recv.at[j - 1, at],
            device_id={"dp": to * GROUP + mine}, device_id_type=MESH,
        )

    def needed(j, tap):
        return overlaps(mine, tap, lax.rem(group + j, groups) * GROUP, GROUP)

    leading = group_tap(lax.rem(group + 1, groups)) // 9
    for k in range(GROUP):
        slot = ([mine] + peers)[k]
        if k == 1:
            send_cotangent(peers[2]).start()
        if k == 0:
            left = hown[row_half(mine), :].astype(jnp.bfloat16)
            shifted_copies(lambda at: gown[at, column_half(mine)], half, narrow)
        else:
            arrived(hin, slot, h_send, h_recv)
            left = hin[slot].astype(jnp.bfloat16)
            arrived(gin, slot, g_send, g_recv)
            shifted_copies(lambda at: gin[slot, at, :], half, narrow)
        for step in range(3):
            a = lax.rem(leading + step, 3)
            at = pl.ds(pl.multiple_of((2 - a) * PLANE, PLANE), vox)
            term = jnp.dot(left, narrow[at, :], preferred_element_type=jnp.float32)
            for bc in range(9):
                piece = term[:, bc * half : (bc + 1) * half]
                if k == 0:
                    parts[a * 9 + bc] = piece
                else:
                    parts[a * 9 + bc] += piece
            if k == GROUP - 1:

                def hand_on(bc, carry):
                    tap = a * 9 + bc
                    for j in range(1, groups):

                        @pl.when(needed(j, tap))
                        def _():
                            handover(j, tap).start()

                    return carry

                lax.fori_loop(0, 9, hand_on, 0)

    def owner_tap(place):
        return (base + place) * rows // chans

    def deliver(u, tap, peer):
        at = tap - owner_tap(peer)
        return pltpu.make_async_remote_copy(
            src_ref=done.at[u],
            dst_ref=final.at[pl.ds(pl.multiple_of(at * chans + lax.rem(mine, 2) * half, half), half), column_half(mine)],
            send_sem=f_send.at[peer, at], recv_sem=f_recv.at[mine, at],
            device_id={"dp": base + peer}, device_id_type=MESH,
        )

    def finish(u, carry):
        tap = group_tap(group) + u

        @pl.when(overlaps(mine, tap, base, GROUP))
        def _():
            value = parts[tap]
            for j in range(1, groups):
                pltpu.make_async_remote_copy(
                    src_ref=parts.at[tap], dst_ref=rbuf.at[j - 1, u],
                    send_sem=p_send.at[j - 1, u], recv_sem=p_recv.at[j - 1, u],
                    device_id={"dp": lax.rem(group + j, groups) * GROUP + mine}, device_id_type=MESH,
                ).wait_recv()
                value = value + rbuf[j - 1, u]
            value = value * (1.0 / n)
            done[u] = value
            for peer in peers:

                @pl.when(overlaps(mine, tap, base + peer, 1))
                def _():
                    deliver(u, tap, peer).start()

            @pl.when(overlaps(mine, tap, me, 1))
            def _():
                at = (tap - owner_tap(mine)) * chans + lax.rem(mine, 2) * half
                final[pl.ds(pl.multiple_of(at, half), half), column_half(mine)] = value

        return carry

    lax.fori_loop(0, reach, finish, 0)

    def collect(at, carry):
        tap = owner_tap(mine) + at
        for peer in peers:

            @pl.when(overlaps(peer, tap, me, 1))
            def _():
                pltpu.make_async_remote_copy(
                    src_ref=done.at[0],
                    dst_ref=final.at[
                        pl.ds(pl.multiple_of(at * chans + lax.rem(peer, 2) * half, half), half), column_half(peer)
                    ],
                    send_sem=f_send.at[peer, at], recv_sem=f_recv.at[peer, at],
                    device_id={"dp": base + peer}, device_id_type=MESH,
                ).wait_recv()

        return carry

    lax.fori_loop(0, span, collect, 0)
    shard_out[0] = final[pl.ds(pl.multiple_of(lax.rem(me * rows, chans), 8), rows), :]

    for peer in peers:
        send_hidden(peer).wait_send()
        send_cotangent(peer).wait_send()

    def drain(tap, carry):
        for j in range(1, groups):

            @pl.when(needed(j, tap))
            def _():
                handover(j, tap).wait_send()

        for peer in peers:

            @pl.when(overlaps(mine, tap, base + peer, 1))
            def _():
                deliver(tap - group_tap(group), tap, peer).wait_send()

        return carry

    lax.fori_loop(0, TAPS, drain, 0)

    @pl.when(level > 0)
    def _():
        chain().wait_send()


def body(acts, out_grad, weights):
    n = lax.axis_size("dp")
    levels = lax.axis_size("section")
    vox, chans = acts.shape[2:]
    half = chans // 2
    rows = TAPS * chans // n
    groups = n // GROUP
    others = max(groups - 1, 1)

    def most(width):
        return max((d + width - 1) // chans - d // chans + 1 for d in range(0, TAPS * chans, width))

    span, reach = most(rows), most(rows * GROUP)
    sems = pltpu.SemaphoreType.DMA
    f32, b16 = jnp.float32, jnp.bfloat16
    return pl.pallas_call(
        functools.partial(kernel, n, levels, rows, span, reach),
        out_shape=(
            jax.ShapeDtypeStruct(acts.shape, f32),
            jax.ShapeDtypeStruct((1, rows, chans), f32),
        ),
        in_specs=[
            pl.BlockSpec(memory_space=pltpu.VMEM),
            pl.BlockSpec(memory_space=pltpu.VMEM),
            pl.BlockSpec(memory_space=pl.ANY),
        ],
        out_specs=(pl.BlockSpec(memory_space=pltpu.VMEM), pl.BlockSpec(memory_space=pltpu.VMEM)),
        scratch_shapes=[
            pltpu.VMEM((chans, TAPS * chans), b16),
            pltpu.VMEM((chans, vox), f32),
            pltpu.VMEM((GROUP, half, vox), f32),
            pltpu.VMEM((vox, chans), f32),
            pltpu.VMEM((GROUP, vox, half), f32),
            pltpu.VMEM((vox + 2 * PLANE, 9 * chans), b16),
            pltpu.VMEM((vox + 2 * PLANE, 9 * half), b16),
            pltpu.VMEM((vox, chans), f32),
            pltpu.VMEM((TAPS, half, half), f32),
            pltpu.VMEM((others, reach, half, half), f32),
            pltpu.VMEM((reach, half, half), f32),
            pltpu.VMEM((span * chans, chans), f32),
            sems((TAPS,)),
            sems((GROUP,)), sems((GROUP,)), sems((GROUP,)), sems((GROUP,)),
            sems, sems,
            sems((others, reach)), sems((others, reach)),
            sems((GROUP, span)), sems((GROUP, span)),
        ],
        compiler_params=pltpu.CompilerParams(
            collective_id=0, has_side_effects=True, vmem_limit_bytes=50 * 1024 * 1024
        ),
        cost_estimate=pl.CostEstimate(flops=4 * 10**9, bytes_accessed=6 * 10**6, transcendentals=vox * chans),
    )(acts, out_grad, weights)


def solution(mesh):
    return jax.shard_map(
        body,
        mesh=mesh,
        in_specs=(
            P("section", "dp", None, None),
            P("dp", None, None),
            P("section", None, None, None),
        ),
        out_specs=(P("section", "dp", None, None), P("section", "dp", None)),
        check_vma=False,
    )
```
